32 devices in a mesh: section: 2 (over core), dp: 4 (over z), tensor: 4 (over y, x).
Axes of the slice: x: 2, y: 2, z: 4, core: 2. Of those that a mesh axis runs over, the one named last changes fastest.
Arguments:
- inputs: bfloat16 [3, 4608, 768], P(None, ('dp', 'tensor')), may hold values from -6 to 6
- cotangent: bfloat16 [3, 4608, 768], P(None, ('dp', 'tensor')), may hold values from -6 to 6
- lengths: int32 [4, 3, 4], P('dp'), may hold values from 1 to 1024, as said below
- ln1_gain: bfloat16 [2, 768], P('section', ('dp', 'tensor')), may hold values from 0.5 to 1.5
- ln1_bias: bfloat16 [2, 768], P('section', ('dp', 'tensor')), may hold values from -1.75 to 1.75
- q_weight: bfloat16 [2, 768, 768], P('section', 'dp', 'tensor'), may hold values from -0.21875 to 0.21875
- q_bias: bfloat16 [2, 12, 64], P('section', 'tensor', 'dp'), may hold values from -3 to 3
- k_weight: bfloat16 [2, 768, 768], P('section', 'dp', 'tensor'), may hold values from -0.21875 to 0.21875
- v_weight: bfloat16 [2, 768, 768], P('section', 'dp', 'tensor'), may hold values from -0.21875 to 0.21875
- v_bias: bfloat16 [2, 12, 64], P('section', 'tensor', 'dp'), may hold values from -3 to 3
- o_weight: bfloat16 [2, 768, 768], P('section', 'tensor', 'dp'), may hold values from -3.5 to 3.5
- o_bias: bfloat16 [2, 768], P('section', ('dp', 'tensor')), may hold values from -1.75 to 1.75
- ln2_gain: bfloat16 [2, 768], P('section', ('dp', 'tensor')), may hold values from 0.5 to 1.5
- ln2_bias: bfloat16 [2, 768], P('section', ('dp', 'tensor')), may hold values from -1.75 to 1.75
- fc1_weight: bfloat16 [2, 768, 3072], P('section', 'dp', 'tensor'), may hold values from -0.21875 to 0.21875
- fc1_bias: bfloat16 [2, 48, 64], P('section', 'tensor', 'dp'), may hold values from -3 to 3
- fc2_weight: bfloat16 [2, 3072, 768], P('section', 'tensor', 'dp'), may hold values from -0.625 to 0.625
- fc2_bias: bfloat16 [2, 768], P('section', ('dp', 'tensor')), may hold values from -1.75 to 1.75
Outputs:
- acts: bfloat16 [2, 3, 4608, 768], P('section', None, ('dp', 'tensor'))
- backs: bfloat16 [2, 3, 4608, 768], P('section', None, ('dp', 'tensor'))
- grad_ln1_gain: float32 [2, 768], P('section', ('dp', 'tensor'))
- grad_ln1_bias: float32 [2, 768], P('section', ('dp', 'tensor'))
- grad_q_weight: float32 [2, 768, 768], P('section', 'dp', 'tensor')
- grad_q_bias: float32 [2, 12, 64], P('section', 'tensor', 'dp')
- grad_k_weight: float32 [2, 768, 768], P('section', 'dp', 'tensor')
- grad_v_weight: float32 [2, 768, 768], P('section', 'dp', 'tensor')
- grad_v_bias: float32 [2, 12, 64], P('section', 'tensor', 'dp')
- grad_o_weight: float32 [2, 768, 768], P('section', 'tensor', 'dp')
- grad_o_bias: float32 [2, 768], P('section', ('dp', 'tensor'))
- grad_ln2_gain: float32 [2, 768], P('section', ('dp', 'tensor'))
- grad_ln2_bias: float32 [2, 768], P('section', ('dp', 'tensor'))
- grad_fc1_weight: float32 [2, 768, 3072], P('section', 'dp', 'tensor')
- grad_fc1_bias: float32 [2, 48, 64], P('section', 'tensor', 'dp')
- grad_fc2_weight: float32 [2, 3072, 768], P('section', 'tensor', 'dp')
- grad_fc2_bias: float32 [2, 768], P('section', ('dp', 'tensor'))
The draws below stay inside these ranges and needn't reach their ends.
Inputs may be any that keep to these rules, and one draw needn't show every extreme that they name: In each row lengths[g, m], one entry is exactly 1024, at a place that varies; the other entries are positive and sum to 128.
All inputs are finite; a program needn't handle non-finite values.
Results may differ from the reference program's by a relative error of at most 0.018.
Values may be sent and summed in bfloat16 or wider, within the bound.
A program may use at most 256 MiB of HBM per device.

```python
import jax
import jax.numpy as jnp
from jax import lax

D = 768
H = 12
HD = 64
FF = 3072
MB = 3
NDOC = 4
DOC_LONG = 1024
REST = 128
LAYERS = 2
GROUPS = 4
TOK_MB = 1152
TOKENS = 4608


def draw_lengths(key, part):
    key = jax.random.fold_in(key, 11)
    key_place, key_units = jax.random.split(key)
    spare_units = REST - (NDOC - 1)
    unit_slots = jax.random.randint(key_units, (GROUPS, MB, spare_units), 0, NDOC - 1)
    slot_ids = jnp.arange(NDOC - 1, dtype=jnp.int32)
    counts = jnp.sum((unit_slots[..., None] == slot_ids).astype(jnp.int32), axis=2) + 1
    long_place = jax.random.randint(key_place, (GROUPS, MB, 1), 0, NDOC)
    columns = jnp.arange(NDOC, dtype=jnp.int32)
    source = jnp.clip(jnp.where(columns < long_place, columns, columns - 1), 0, NDOC - 2)
    source = jnp.broadcast_to(source, (GROUPS, MB, NDOC)).astype(jnp.int32)
    picked = jnp.take_along_axis(counts, source, axis=2)
    return jnp.where(columns == long_place, DOC_LONG, picked).astype(jnp.int32)


def levels(key, shape, shards, least, high):
    level, own = 1.0, jax.random.fold_in(key, 6)
    for dim, blocks in shards:
        draws = jnp.exp(jax.random.uniform(jax.random.fold_in(own, dim), (blocks,), jnp.float32, least / len(shards), high / len(shards)))
        level = level * jnp.repeat(draws, shape[dim] // blocks).reshape([-1 if axis == dim else 1 for axis in range(len(shape))])
    return level


def scatter_about(rng, shape, width, bound, shards=(), kind=jnp.bfloat16):
    drawn = jax.random.normal(rng, shape, jnp.float32) * width
    if len(shards) > 0:
        drawn = levels(rng, shape, shards, -0.22, 0.18) * drawn
    return jnp.clip(drawn, min=-bound, max=bound).astype(kind)


def setup_inputs(seed: int = 0) -> dict:
    key_of = jax.random.split(jax.random.key(seed), 19)
    return {
        "inputs": scatter_about(key_of[0], (MB, TOKENS, D), 1.0, 6.0, ((1, 16),)),
        "cotangent": scatter_about(key_of[1], (MB, TOKENS, D), 1.0, 6.0, ((1, 16),)),
        "lengths": draw_lengths(jax.random.fold_in(key_of[18], 71), 0),
        "ln1_gain": jnp.clip(1.0 + 0.1 * jax.random.normal(key_of[3], (LAYERS, D), jnp.float32), 0.5, 1.5).astype(jnp.bfloat16),
        "ln1_bias": scatter_about(key_of[4], (LAYERS, D), 0.3, 1.75, ((0, 2), (1, 16))),
        "q_weight": scatter_about(key_of[5], (LAYERS, D, D), D ** -0.5, 0.21875, ((0, 2), (1, 4), (2, 4))),
        "q_bias": scatter_about(key_of[6], (LAYERS, H, HD), 0.5, 3.0, ((0, 2), (1, 4), (2, 4))),
        "k_weight": scatter_about(key_of[7], (LAYERS, D, D), D ** -0.5, 0.21875, ((0, 2), (1, 4), (2, 4))),
        "v_weight": scatter_about(key_of[8], (LAYERS, D, D), D ** -0.5, 0.21875, ((0, 2), (1, 4), (2, 4))),
        "v_bias": scatter_about(key_of[9], (LAYERS, H, HD), 0.5, 3.0, ((0, 2), (1, 4), (2, 4))),
        "o_weight": scatter_about(key_of[10], (LAYERS, D, D), (max(D // 256, 1)) ** -0.5, 3.5, ((0, 2), (1, 4), (2, 4))),
        "o_bias": scatter_about(key_of[11], (LAYERS, D), 0.3, 1.75, ((0, 2), (1, 16))),
        "ln2_gain": jnp.clip(1.0 + 0.1 * jax.random.normal(key_of[12], (LAYERS, D), jnp.float32), 0.5, 1.5).astype(jnp.bfloat16),
        "ln2_bias": scatter_about(key_of[13], (LAYERS, D), 0.3, 1.75, ((0, 2), (1, 16))),
        "fc1_weight": scatter_about(key_of[14], (LAYERS, D, FF), D ** -0.5, 0.21875, ((0, 2), (1, 4), (2, 4))),
        "fc1_bias": scatter_about(key_of[15], (LAYERS, FF // HD, HD), 0.5, 3.0, ((0, 2), (1, 4), (2, 4))),
        "fc2_weight": scatter_about(key_of[16], (LAYERS, FF, D), (max(FF // 32, 1)) ** -0.5, 0.625, ((0, 2), (1, 4), (2, 4))),
        "fc2_bias": scatter_about(key_of[17], (LAYERS, D), 0.3, 1.75, ((0, 2), (1, 16))),
    }


@jax.custom_vjp
def low(v):
    return lax.optimization_barrier(v.astype(jnp.bfloat16)).astype(jnp.float32)

@jax.custom_vjp
def low_back(v):
    return v

def low_keep(v):
    return (low(v), None)

def low_pass(kept, grad):
    return (grad,)

def back_keep(v):
    return (v, None)

def back_low(kept, grad):
    return (low(grad),)
low.defvjp(low_keep, low_pass)
low_back.defvjp(back_keep, back_low)
EPSILON = 1e-05
HIGH = lax.Precision.HIGHEST

def matmul(left, right):
    return jnp.dot(left, right, precision=HIGH, preferred_element_type=jnp.float32)

def normalize(values, scale_vec, shift_vec):
    center = values - lax.optimization_barrier(jnp.mean(values, axis=-1, keepdims=True))
    spread = lax.optimization_barrier(jnp.mean(center * center, axis=-1, keepdims=True))
    return center * lax.rsqrt(spread + EPSILON) * scale_vec + shift_vec

def doc_mask(length_row, row_count):
    doc_ends = jnp.cumsum(length_row).astype(jnp.int32)
    places = jnp.arange(row_count, dtype=jnp.int32)
    doc_ids = lax.optimization_barrier(jnp.sum((places[:, None] >= doc_ends[None, :]).astype(jnp.int32), axis=1))
    same_doc = doc_ids[:, None] == doc_ids[None, :]
    causal = places[None, :] <= places[:, None]
    return same_doc & causal

def layer(hidden, params, allowed):
    ln1_gain, ln1_bias, q_weight, q_bias, k_weight, v_weight, v_bias, o_weight, o_bias, ln2_gain, ln2_bias, fc1_weight, fc1_bias, fc2_weight, fc2_bias = params
    row_count = hidden.shape[0]
    head_count = q_bias.shape[0]
    head_size = q_bias.shape[1]
    normed = low(normalize(hidden, ln1_gain, ln1_bias))
    queries = low_back(low(matmul(normed, q_weight) + q_bias.reshape(-1)))
    key_rows = low_back(low(matmul(normed, k_weight)))
    values = low_back(low(matmul(normed, v_weight) + v_bias.reshape(-1)))
    query_heads = queries.reshape(row_count, head_count, head_size)
    key_heads = key_rows.reshape(row_count, head_count, head_size)
    value_heads = values.reshape(row_count, head_count, head_size)
    scores = jnp.einsum('qhd,khd->hqk', query_heads, key_heads, precision=HIGH)
    scores = low_back(scores * head_size ** (-0.5))
    scores = jnp.where(allowed[None], scores, -1e+30)
    row_top = lax.optimization_barrier(jnp.max(scores, axis=-1, keepdims=True))
    exponent = jnp.exp(scores - row_top)
    attention = exponent / lax.optimization_barrier(jnp.sum(exponent, axis=-1, keepdims=True))
    mixed = jnp.einsum('hqk,khd->qhd', low(attention), value_heads, precision=HIGH)
    mixed = low_back(low(mixed.reshape(row_count, head_count * head_size)))
    branch = low_back(matmul(mixed, o_weight))
    middle = hidden + branch + o_bias
    normed_two = low(normalize(middle, ln2_gain, ln2_bias))
    hidden_pre = low_back(matmul(normed_two, fc1_weight) + fc1_bias.reshape(-1))
    active = low(jax.nn.gelu(hidden_pre, approximate=True))
    branch_two = low_back(matmul(active, fc2_weight))
    return middle + branch_two + fc2_bias

def reference(inputs, cotangent, lengths, ln1_gain, ln1_bias, q_weight, q_bias, k_weight, v_weight, v_bias, o_weight, o_bias, ln2_gain, ln2_bias, fc1_weight, fc1_bias, fc2_weight, fc2_bias):
    weight_list = (ln1_gain, ln1_bias, q_weight, q_bias, k_weight, v_weight, v_bias, o_weight, o_bias, ln2_gain, ln2_bias, fc1_weight, fc1_bias, fc2_weight, fc2_bias)
    first = tuple((element[0].astype(jnp.float32) for element in weight_list))
    second = tuple((element[1].astype(jnp.float32) for element in weight_list))
    rows_in = inputs.reshape(MB * GROUPS, TOK_MB, D)
    rows_cot = cotangent.reshape(MB * GROUPS, TOK_MB, D)
    length_rows = jnp.transpose(lengths, (1, 0, 2)).reshape(MB * GROUPS, NDOC)
    zeros = jax.tree.map(jnp.zeros_like, (first, second))

    def visit(totals, element):
        source, grad_out, length_row = element
        allowed = doc_mask(length_row, TOK_MB)

        def run(hidden, params):
            return layer(hidden, params, allowed)
        out_one, pull_one = jax.vjp(run, source.astype(jnp.float32), first)
        act_one = out_one.astype(jnp.bfloat16)
        out_two, pull_two = jax.vjp(run, act_one.astype(jnp.float32), second)
        act_two = out_two.astype(jnp.bfloat16)
        back_two, grads_two = pull_two(grad_out.astype(jnp.float32))
        back_two = back_two.astype(jnp.bfloat16)
        back_one, grads_one = pull_one(back_two.astype(jnp.float32))
        totals = jax.tree.map(lambda left, right: left + right, totals, (grads_one, grads_two))
        return (totals, (act_one, act_two, back_one.astype(jnp.bfloat16), back_two))
    totals, outputs = lax.scan(visit, zeros, (rows_in, rows_cot, length_rows))
    act_one, act_two, back_one, back_two = outputs
    acts = jnp.stack([act_one, act_two]).reshape(LAYERS, MB, TOKENS, D)
    backs = jnp.stack([back_one, back_two]).reshape(LAYERS, MB, TOKENS, D)
    grads = tuple((jnp.stack([totals[0][number], totals[1][number]]) for number in range(15)))
    return (acts, backs, grads[0], grads[1], grads[2], grads[3], grads[4], grads[5], grads[6], grads[7], grads[8], grads[9], grads[10], grads[11], grads[12], grads[13], grads[14])
```

```python
import jax
import jax.numpy as jnp
from jax import lax
from jax.sharding import PartitionSpec as P

HD = 64
EPSILON = 1e-05
MASKED = -1e30
ALL = ("dp", "tensor")


def swap(array):
    return lax.ppermute(array, "section", [(0, 1), (1, 0)])


def normalize(values, scale_vec, shift_vec):
    center = values - jnp.mean(values, axis=-1, keepdims=True)
    spread = jnp.mean(center * center, axis=-1, keepdims=True)
    return center * lax.rsqrt(spread + EPSILON) * scale_vec + shift_vec


def plain(left, right):
    return jnp.dot(left, right, preferred_element_type=jnp.float32)


def contract_rows(left, right):
    return lax.dot_general(
        left, right, (((0,), (0,)), ((), ())), preferred_element_type=jnp.float32
    )


def contract_cols(left, right):
    return lax.dot_general(
        left, right, (((1,), (1,)), ((), ())), preferred_element_type=jnp.float32
    )


def heads_of(array):
    return array.reshape(array.shape[0], -1, HD)


def scores_of(queries, keys, rows):
    starts, places, key_places = rows
    scores = jnp.einsum(
        "qhd,khd->hqk", heads_of(queries), heads_of(keys), preferred_element_type=jnp.float32
    ) * HD ** (-0.5)
    allowed = (key_places >= starts) & (key_places <= places)
    return jnp.where(allowed[None], scores, MASKED)


def attend(queries, keys, values, rows):
    scores = scores_of(queries, keys, rows)
    row_top = jnp.max(scores, axis=-1, keepdims=True)
    exponent = jnp.exp(scores - row_top)
    row_total = jnp.sum(exponent, axis=-1, keepdims=True)
    probs = (exponent / row_total).astype(jnp.bfloat16)
    mixed = jnp.einsum("hqk,khd->qhd", probs, heads_of(values), preferred_element_type=jnp.float32)
    return mixed.reshape(queries.shape).astype(jnp.bfloat16), row_top + jnp.log(row_total)


def attend_back(queries, keys, values, rows, log_total, grad_mixed):
    probs = jnp.exp(scores_of(queries, keys, rows) - log_total)
    grads = heads_of(grad_mixed)
    grad_probs = jnp.einsum(
        "qhd,khd->hqk", grads, heads_of(values), preferred_element_type=jnp.float32
    )
    grad_values = jnp.einsum(
        "hqk,qhd->khd", probs.astype(jnp.bfloat16), grads, preferred_element_type=jnp.float32
    )
    row_delta = jnp.sum(probs * grad_probs, axis=-1, keepdims=True)
    grad_scores = (probs * (grad_probs - row_delta)).astype(jnp.bfloat16)
    grad_queries = (
        jnp.einsum("hqk,khd->qhd", grad_scores, heads_of(keys), preferred_element_type=jnp.float32)
        * HD ** (-0.5)
    )
    grad_keys = (
        jnp.einsum(
            "hqk,qhd->khd", grad_scores, heads_of(queries), preferred_element_type=jnp.float32
        )
        * HD ** (-0.5)
    )
    return tuple(
        element.reshape(element.shape[0], -1) for element in (grad_queries, grad_keys, grad_values)
    )


def forward_layer(source, rows, weights, vectors):
    qkv_weight, o_weight, fc1_weight, fc2_weight = weights
    ln1_gain, ln1_bias, o_bias, ln2_gain, ln2_bias, fc2_bias, q_bias, v_bias, fc1_bias = vectors
    width = source.shape[1]
    hidden = source.astype(jnp.float32)
    normed = normalize(hidden, ln1_gain, ln1_bias).astype(jnp.bfloat16)
    qkv_bias = jnp.concatenate([q_bias, jnp.zeros_like(q_bias), v_bias])
    qkv = (plain(normed, qkv_weight) + qkv_bias).astype(jnp.bfloat16)
    queries, own = qkv[:, :width], qkv[:, width:]
    both = jnp.concatenate([own, swap(own)], axis=0)
    keys, values = both[:, :width], both[:, width:]
    mixed, log_total = attend(queries, keys, values, rows)
    middle = hidden + contract_cols(mixed, o_weight) + o_bias
    normed_two = normalize(middle, ln2_gain, ln2_bias).astype(jnp.bfloat16)
    hidden_pre = plain(normed_two, fc1_weight) + fc1_bias
    active = jax.nn.gelu(hidden_pre, approximate=True).astype(jnp.bfloat16)
    result = middle + contract_cols(active, fc2_weight) + fc2_bias
    saved = (
        hidden, middle, normed, queries, keys, values, log_total, mixed, normed_two, hidden_pre,
        active,
    )
    return result.astype(jnp.bfloat16), saved


def backward_layer(grad_out, rows, weights, vectors, saved):
    qkv_weight, o_weight, fc1_weight, fc2_weight = weights
    ln1_gain, ln1_bias, o_bias, ln2_gain, ln2_bias, fc2_bias, q_bias, v_bias, fc1_bias = vectors
    (
        hidden, middle, normed, queries, keys, values, log_total, mixed, normed_two, hidden_pre,
        active,
    ) = saved
    count, width = hidden.shape
    grad_mlp = grad_out.astype(jnp.bfloat16)
    grad_fc2 = contract_rows(grad_mlp, active)
    grad_fc2_bias = jnp.sum(grad_out, axis=0)
    gelu_value, gelu_pull = jax.vjp(lambda inner: jax.nn.gelu(inner, approximate=True), hidden_pre)
    grad_pre = gelu_pull(plain(grad_mlp, fc2_weight))[0].astype(jnp.bfloat16)
    grad_fc1_bias = jnp.sum(grad_pre, axis=0, dtype=jnp.float32)
    grad_fc1 = contract_rows(normed_two, grad_pre)
    norm_value, norm_pull = jax.vjp(normalize, middle, ln2_gain, ln2_bias)
    grad_middle, grad_ln2_gain, grad_ln2_bias = norm_pull(contract_cols(grad_pre, fc1_weight))
    grad_middle = grad_middle + grad_out
    grad_o_bias = jnp.sum(grad_middle, axis=0)
    grad_branch = grad_middle.astype(jnp.bfloat16)
    grad_o = contract_rows(grad_branch, mixed)
    grad_mixed = plain(grad_branch, o_weight).astype(jnp.bfloat16)
    grad_queries, grad_keys, grad_values = attend_back(
        queries, keys, values, rows, log_total, grad_mixed
    )
    grad_both = jnp.concatenate([grad_keys, grad_values], axis=1)
    arrived = swap(grad_both[count:].astype(jnp.bfloat16))
    grad_own = grad_both[:count] + arrived.astype(jnp.float32)
    grad_qkv = jnp.concatenate([grad_queries, grad_own], axis=1).astype(jnp.bfloat16)
    grad_qkv_bias = jnp.sum(grad_qkv, axis=0, dtype=jnp.float32)
    grad_qkv_weight = contract_rows(normed, grad_qkv)
    first_value, first_pull = jax.vjp(normalize, hidden, ln1_gain, ln1_bias)
    grad_hidden, grad_ln1_gain, grad_ln1_bias = first_pull(contract_cols(grad_qkv, qkv_weight))
    grad_hidden = grad_hidden + grad_middle
    vector_terms = (
        grad_ln1_gain, grad_ln1_bias, grad_o_bias, grad_ln2_gain, grad_ln2_bias, grad_fc2_bias,
        grad_qkv_bias[:width], grad_qkv_bias[2 * width :], grad_fc1_bias,
    )
    return (
        grad_hidden.astype(jnp.bfloat16),
        vector_terms,
        (grad_qkv_weight, grad_o, grad_fc1, grad_fc2),
    )


def local(
    inputs, cotangent, lengths, ln1_gain, ln1_bias, q_weight, q_bias, k_weight, v_weight, v_bias,
    o_weight, o_bias, ln2_gain, ln2_bias, fc1_weight, fc1_bias, fc2_weight, fc2_bias,
):
    first = lax.axis_index("section") == 0
    dp, tensor = lax.axis_size("dp"), lax.axis_size("tensor")
    peers = dp * tensor
    micro_count, chunk, width = inputs.shape
    assert micro_count <= tensor
    assert tensor % 4 == 0
    depth = q_weight.shape[1]
    heads_wide = q_weight.shape[2]
    units = fc1_weight.shape[2]
    assert units == 4 * heads_wide

    def pick(own, other):
        return jnp.where(first, own, other), jnp.where(first, other, own)

    attention_block = jnp.concatenate(
        [q_weight[0], k_weight[0], v_weight[0], o_weight[0].T], axis=1
    )
    packed = jnp.stack([attention_block, fc1_weight[0], fc2_weight[0].T])
    packed = packed.reshape(3, 2, depth // 2, units)
    small = jnp.concatenate(
        [
            element.reshape(-1)
            for element in (
                ln1_gain, ln1_bias, o_bias, ln2_gain, ln2_bias, fc2_bias, q_bias, v_bias, fc1_bias,
            )
        ]
    )
    small_size = small.shape[0]
    small_rows = -(-small_size // 2048) * 16
    small = jnp.pad(small, (0, small_rows * 128 - small_size)).reshape(small_rows, 128)
    packed_layers = pick(packed, swap(packed))
    small_all = lax.all_gather(small, ALL, axis=0)
    small_layers = pick(small_all, swap(small_all))

    def gather_half(blocks):
        mine = jnp.where(first, blocks[:, 0], blocks[:, 1])
        got = lax.all_gather(mine, ALL, axis=0)
        halves = pick(got, swap(got))
        return jnp.stack(halves, axis=2).reshape(dp, tensor, blocks.shape[0], depth, units)

    def attention_weights(layer):
        blocks = gather_half(packed_layers[layer][:1])[:, :, 0]
        blocks = blocks.reshape(dp, tensor, depth, 4, heads_wide)
        qkv = blocks[:, :, :, :3].transpose(0, 2, 3, 1, 4).reshape(dp * depth, -1)
        out = blocks[:, :, :, 3].transpose(0, 2, 1, 3).reshape(dp * depth, -1)
        return qkv, out

    def mlp_weights(layer):
        blocks = gather_half(packed_layers[layer][1:])
        return tuple(
            blocks[:, :, i].transpose(0, 2, 1, 3).reshape(dp * depth, -1) for i in range(2)
        )

    slice_width = width // peers
    head_local, head_part = q_bias.shape[1], q_bias.shape[2]
    unit_rows = fc1_bias.shape[1]

    def vectors_of(layer):
        flat = small_layers[layer].reshape(peers, -1)[:, :small_size].astype(jnp.float32)
        six = [flat[:, i * slice_width : (i + 1) * slice_width].reshape(-1) for i in range(6)]
        place = 6 * slice_width
        rest = []
        for rows in (head_local, head_local, unit_rows):
            part = flat[:, place : place + rows * head_part].reshape(dp, tensor, rows, head_part)
            rest.append(part.transpose(1, 2, 0, 3).reshape(-1))
            place += rows * head_part
        return six + rest

    order = (
        [i for i in range(tensor) if i % 4 in (0, 3)],
        [i for i in range(tensor) if i % 4 in (1, 2)],
    )
    spare = tensor - micro_count
    pair = jnp.pad(jnp.stack([inputs, cotangent], axis=1), ((0, spare), (0, 0), (0, 0), (0, 0)))
    pair = lax.all_to_all(pair, "tensor", 0, 0, tiled=True)

    def own_rows(array):
        return jnp.where(
            first,
            jnp.concatenate([array[i] for i in order[0]], axis=0),
            jnp.concatenate([array[i] for i in order[1]], axis=0),
        )

    source, given = own_rows(pair[:, 0]), own_rows(pair[:, 1])

    places_two = [
        jnp.concatenate([jnp.arange(chunk, dtype=jnp.int32) + i * chunk for i in part])
        for part in order
    ]
    own_places, other_places = pick(places_two[0], places_two[1])
    micro = jnp.minimum(lax.axis_index("tensor"), micro_count - 1)
    ends = jnp.cumsum(lax.dynamic_index_in_dim(lengths[0], micro, 0, keepdims=False))
    starts = jnp.max(
        jnp.where(own_places[:, None] >= ends[None, :], ends[None, :], 0), axis=1, keepdims=True
    )
    rows = (starts, own_places[:, None], jnp.concatenate([own_places, other_places])[None, :])

    weights, vectors = [], []
    for layer in range(2):
        weights.append(attention_weights(layer) + mlp_weights(layer))
        vectors.append(vectors_of(layer))
    act_zero, saved_zero = forward_layer(source, rows, weights[0], vectors[0])
    act_one, saved_one = forward_layer(act_zero, rows, weights[1], vectors[1])

    def hand_out(zero, one):
        keep, send = pick(zero, one)
        core_zero, core_one = pick(keep, swap(send))
        pieces = [None] * tensor
        for part, array in zip(order, (core_zero, core_one)):
            for i, piece in zip(part, jnp.split(array, len(part), axis=0)):
                pieces[i] = piece
        spread = lax.all_to_all(jnp.stack(pieces), "tensor", 0, 0, tiled=True)
        return spread[:micro_count][None]

    def reduce_weights(terms):
        grad_qkv, grad_o, grad_fc1, grad_fc2 = [term.astype(jnp.bfloat16) for term in terms]
        qkv = grad_qkv.reshape(dp, depth, 3, tensor, heads_wide)
        out = grad_o.reshape(dp, depth, 1, tensor, heads_wide)
        attention = jnp.concatenate([qkv, out], axis=2).transpose(0, 3, 1, 2, 4)
        attention = attention.reshape(dp, tensor, depth, units)
        fc1 = grad_fc1.reshape(dp, depth, tensor, units).transpose(0, 2, 1, 3)
        fc2 = grad_fc2.reshape(dp, depth, tensor, units).transpose(0, 2, 1, 3)

        def scatter(blocks):
            halves = blocks.reshape(peers, 2, depth // 2, units)
            keep, send = pick(halves[:, 0], halves[:, 1])
            total = keep.astype(jnp.float32) + swap(send).astype(jnp.float32)
            total = total.astype(jnp.bfloat16)
            return lax.psum_scatter(total, ALL, scatter_dimension=0, tiled=True)[0]

        return jnp.stack([scatter(fc2), scatter(fc1), scatter(attention)])

    def small_terms(terms):
        flat = [term.reshape(peers, -1) for term in terms[:6]]
        for term in terms[6:]:
            part = term.reshape(tensor, -1, dp, head_part).transpose(2, 0, 1, 3)
            flat.append(part.reshape(peers, -1))
        flat = jnp.concatenate(flat, axis=1)
        return jnp.pad(flat, ((0, 0), (0, small_rows * 128 - small_size)))

    grad_one = given.astype(jnp.float32)
    back_one, small_one, large_one = backward_layer(
        grad_one, rows, weights[1], vectors[1], saved_one
    )
    shard_one = reduce_weights(large_one)
    back_zero, small_zero, large_zero = backward_layer(
        back_one.astype(jnp.float32), rows, weights[0], vectors[0], saved_zero
    )
    shard_zero = reduce_weights(large_zero)
    acts = hand_out(act_zero, act_one)
    backs = hand_out(back_zero, back_one)

    keep, send = pick(small_terms(small_zero), small_terms(small_one))
    small_sum = (keep + swap(send)).reshape(peers, small_rows, 128)
    small_sum = lax.psum_scatter(small_sum, ALL, scatter_dimension=0, tiled=True)
    small_sum = small_sum.reshape(-1)[:small_size]
    keep, send = pick(shard_zero, shard_one)
    halves = pick(keep, swap(send))
    shard = jnp.concatenate(halves, axis=1).astype(jnp.float32)
    grad_fc2 = shard[0].T
    grad_fc1 = shard[1]
    grad_q, grad_k, grad_v, grad_o = jnp.split(shard[2], 4, axis=1)
    grad_o = grad_o.T
    six = [small_sum[i * slice_width : (i + 1) * slice_width][None] for i in range(6)]
    place = 6 * slice_width
    rest = []
    for count in (head_local, head_local, unit_rows):
        part = small_sum[place : place + count * head_part]
        rest.append(part.reshape(1, count, head_part))
        place += count * head_part
    return (
        acts, backs, six[0], six[1], grad_q[None], rest[0], grad_k[None], grad_v[None], rest[1],
        grad_o[None], six[2], six[3], six[4], grad_fc1[None], rest[2], grad_fc2[None], six[5],
    )


def solution(mesh):
    return jax.shard_map(
        local,
        mesh=mesh,
        in_specs=(
            P(None, ("dp", "tensor"), None),
            P(None, ("dp", "tensor"), None),
            P("dp", None, None),
            P("section", ("dp", "tensor")),
            P("section", ("dp", "tensor")),
            P("section", "dp", "tensor"),
            P("section", "tensor", "dp"),
            P("section", "dp", "tensor"),
            P("section", "dp", "tensor"),
            P("section", "tensor", "dp"),
            P("section", "tensor", "dp"),
            P("section", ("dp", "tensor")),
            P("section", ("dp", "tensor")),
            P("section", ("dp", "tensor")),
            P("section", "dp", "tensor"),
            P("section", "tensor", "dp"),
            P("section", "tensor", "dp"),
            P("section", ("dp", "tensor")),
        ),
        out_specs=(
            P("section", None, ("dp", "tensor"), None),
            P("section", None, ("dp", "tensor"), None),
            P("section", ("dp", "tensor")),
            P("section", ("dp", "tensor")),
            P("section", "dp", "tensor"),
            P("section", "tensor", "dp"),
            P("section", "dp", "tensor"),
            P("section", "dp", "tensor"),
            P("section", "tensor", "dp"),
            P("section", "tensor", "dp"),
            P("section", ("dp", "tensor")),
            P("section", ("dp", "tensor")),
            P("section", ("dp", "tensor")),
            P("section", "dp", "tensor"),
            P("section", "tensor", "dp"),
            P("section", "tensor", "dp"),
            P("section", ("dp", "tensor")),
        ),
        check_vma=False,
    )
```
